32 devices in a mesh: group: 2 (over y), tile: 16 (over z, x, core).
Axes of the slice: x: 2, y: 2, z: 4, core: 2. Of those that a mesh axis runs over, the one named last changes fastest.
Arguments:
- vorticity: float32 [16, 1024, 1024], P(None, ('group', 'tile')), may hold values from -6 to 6
- layer_to_mode: float32 [16, 16], replicated, may hold values from -1.5 to 1.5
- mode_to_layer: float32 [16, 16], replicated, may hold values from -1.5 to 1.5
- inverse_radii: float32 [16], replicated, may hold values from 0.001 to 1
- wind_curl: float32 [1024, 1024], P(('group', 'tile')), may hold values from -6 to 6
- wet_mask: int32 [1024, 1024], P(('group', 'tile')), may hold values 0 or 1
Outputs:
- new_vorticity: float32 [16, 1024, 1024], P(None, ('group', 'tile'))
- stream: float32 [16, 1024, 1024], P(None, ('group', 'tile'))
The draws below stay inside these ranges and needn't reach their ends.
All inputs are finite; a program needn't handle non-finite values. No bound on the sum of `wet_mask` on one device may be relied on, other than what follows from the above.
Results may differ from the reference program's by a relative error of at most 0.00011.
Values sent between devices are 32-bit elements; how exact they have to be, the bound alone decides.
A program may use at most 64 MiB of HBM per device.

```python
import math
import jax
import jax.numpy as jnp
from jax import lax

N = 1024
NL = 16


def touch_ends(array, stream_key, low, largest):
    index_at = [jax.random.randint(jax.random.fold_in(stream_key, axis), (), 0, length) for axis, length in enumerate(array.shape)]
    widest = array.shape.index(max(array.shape))
    next_to = index_at[:widest] + [(index_at[widest] + 1) % array.shape[widest]] + index_at[widest + 1:]
    return array.at[tuple(index_at)].set(low).at[tuple(next_to)].set(largest)


def block_scale(key, dims, pieces, smallest, top_value):
    gain = 1.0
    for position, shards_of in pieces:
        heights = jax.random.uniform(jax.random.fold_in(jax.random.fold_in(key, 6), position), (shards_of,), jnp.float32, smallest / len(pieces), top_value / len(pieces))
        gain = gain * jnp.repeat(jnp.exp(heights), dims[position] // shards_of).reshape((-1,) + (1,) * (len(dims) - 1 - position))
    return gain


def centred(stream_key, extent, width, reach, cuts=(), kind=jnp.bfloat16):
    loudness = block_scale(stream_key, extent, cuts, -0.22, 0.18) if cuts else 1.0
    result = jax.random.normal(stream_key, extent, jnp.float32) * width * loudness
    return jnp.minimum(jnp.maximum(result, -reach), reach).astype(kind)


def setup_inputs(seed: int = 0) -> dict:
    key_of = jax.random.split(jax.random.key(seed), 7)
    vorticity = centred(key_of[0], (NL, N, N), 1.0, 6.0, ((1, 32),), jnp.float32)
    layer_to_mode = centred(key_of[1], (NL, NL), NL ** -0.5, 1.5, (), jnp.float32)
    mode_to_layer = centred(key_of[2], (NL, NL), NL ** -0.5, 1.5, (), jnp.float32)
    inverse_radii = jnp.clip(jnp.exp(jax.random.uniform(key_of[3], (NL,), jnp.float32, math.log(0.001), math.log(1.0))), 0.001, 1.0)
    wind_curl = centred(key_of[4], (N, N), 1.0, 6.0, ((0, 32),), jnp.float32)
    wet_mask = touch_ends((jax.random.randint(key_of[5], (N, N), 0, 10) < 9).astype(jnp.int32), jax.random.fold_in(key_of[5], 1), 0, 1)
    return {"vorticity": vorticity, "layer_to_mode": layer_to_mode, "mode_to_layer": mode_to_layer, "inverse_radii": inverse_radii, "wind_curl": wind_curl, "wet_mask": wet_mask}


time_step = 0.5
beta_plane = 1.0
bottom_drag = 0.2

def make_table(length, positions):
    wavenumber = jnp.arange(length, dtype=jnp.int32) + 1
    phase_index = wavenumber[:, None] * (positions[None, :] + 1) % (2 * (length + 1))
    return math.sqrt(2.0 / (length + 1)) * jnp.sin(math.pi * phase_index.astype(jnp.float32) / (length + 1))

def eigen_values(length, positions):
    return 4.0 * jnp.sin(math.pi * (positions + 1).astype(jnp.float32) / (2 * (length + 1))) ** 2

def matmul(matrix, operand):
    return jnp.dot(matrix, operand, precision=lax.Precision.HIGHEST, preferred_element_type=jnp.float32)

def offset_view(padded, row_step, column_step):
    height = padded.shape[1] - 2
    breadth = padded.shape[2] - 2
    return padded[:, 1 + row_step:1 + row_step + height, 1 + column_step:1 + column_step + breadth]

def tendency_of(vortex_pad, stream_pad, wind_curl):
    vortex_north = offset_view(vortex_pad, 1, 0)
    vortex_south = offset_view(vortex_pad, -1, 0)
    vortex_east = offset_view(vortex_pad, 0, 1)
    vortex_west = offset_view(vortex_pad, 0, -1)
    vortex_northeast = offset_view(vortex_pad, 1, 1)
    vortex_northwest = offset_view(vortex_pad, 1, -1)
    vortex_southeast = offset_view(vortex_pad, -1, 1)
    vortex_southwest = offset_view(vortex_pad, -1, -1)
    stream_mid = offset_view(stream_pad, 0, 0)
    stream_north = offset_view(stream_pad, 1, 0)
    stream_south = offset_view(stream_pad, -1, 0)
    stream_east = offset_view(stream_pad, 0, 1)
    stream_west = offset_view(stream_pad, 0, -1)
    stream_northeast = offset_view(stream_pad, 1, 1)
    stream_northwest = offset_view(stream_pad, 1, -1)
    stream_southeast = offset_view(stream_pad, -1, 1)
    stream_southwest = offset_view(stream_pad, -1, -1)
    arakawa_one = (stream_east - stream_west) * (vortex_north - vortex_south) - (stream_north - stream_south) * (vortex_east - vortex_west)
    arakawa_two = stream_east * (vortex_northeast - vortex_southeast) - stream_west * (vortex_northwest - vortex_southwest) - stream_north * (vortex_northeast - vortex_northwest) + stream_south * (vortex_southeast - vortex_southwest)
    arakawa_three = vortex_north * (stream_northeast - stream_northwest) - vortex_south * (stream_southeast - stream_southwest) - vortex_east * (stream_northeast - stream_southeast) + vortex_west * (stream_northwest - stream_southwest)
    jacobian = (arakawa_one + arakawa_two + arakawa_three) / 12.0
    laplace = stream_north + stream_south + stream_east + stream_west - 4.0 * stream_mid
    layers = stream_mid.shape[0]
    layer_index = jnp.arange(layers, dtype=jnp.int32)
    top_layer = (layer_index == 0).astype(jnp.float32)[:, None, None]
    bottom_layer = (layer_index == layers - 1).astype(jnp.float32)[:, None, None]
    return -jacobian - beta_plane * 0.5 * (stream_east - stream_west) + top_layer * wind_curl[None] - bottom_drag * bottom_layer * laplace

def reference(vorticity, layer_to_mode, mode_to_layer, inverse_radii, wind_curl, wet_mask):
    length = vorticity.shape[-1]
    positions = jnp.arange(length, dtype=jnp.int32)
    sine = make_table(length, positions)
    eigens = eigen_values(length, positions)
    modal_field = jnp.einsum('ml,lyx->myx', layer_to_mode, vorticity, precision=lax.Precision.HIGHEST)

    def invert(operands):
        plane_field, radius = operands
        spectrum = matmul(matmul(sine, plane_field), sine)
        spectrum = -spectrum / (eigens[:, None] + eigens[None, :] + radius)
        return matmul(matmul(sine, spectrum), sine)
    stream_modes = lax.map(invert, (modal_field, inverse_radii))
    stream = jnp.einsum('lm,myx->lyx', mode_to_layer, stream_modes, precision=lax.Precision.HIGHEST)
    padding = ((0, 0), (1, 1), (1, 1))
    tendency = tendency_of(jnp.pad(vorticity, padding), jnp.pad(stream, padding), wind_curl)
    return (vorticity + time_step * wet_mask.astype(jnp.float32) * tendency, stream)
```

```python
import functools
import math

import jax
import jax.numpy as jnp
import ml_dtypes
import numpy as np
from jax import lax
from jax.experimental import pallas as pl
from jax.experimental.pallas import tpu as pltpu
from jax.sharding import PartitionSpec as P

time_step = 0.5
beta_plane = 1.0
bottom_drag = 0.2
MESH = pl.DeviceIdType.MESH
VMEM = pl.BlockSpec(memory_space=pltpu.VMEM)
SMEM = pl.BlockSpec(memory_space=pltpu.SMEM)


def sine_parts(length):
    wave = np.arange(length, dtype=np.int64) + 1
    phase = (wave[:, None] * wave[None, :]) % (2 * (length + 1))
    table = math.sqrt(2.0 / (length + 1)) * np.sin(math.pi * phase / (length + 1))
    high = table.astype(np.float32).astype(ml_dtypes.bfloat16)
    low = (table - high.astype(np.float64)).astype(np.float32).astype(ml_dtypes.bfloat16)
    return high, low


def eigen_values(length):
    wave = np.arange(length, dtype=np.float64) + 1
    return (4.0 * np.sin(math.pi * wave / (2 * (length + 1))) ** 2).astype(np.float32)


def halves(value):
    high = value.astype(jnp.bfloat16)
    low = (value - high.astype(jnp.float32)).astype(jnp.bfloat16)
    return high, low


def dot(left, right):
    return jnp.dot(left, right, preferred_element_type=jnp.float32)


def dot3(left, right):
    (left_high, left_low), (right_high, right_low) = left, right
    return dot(left_high, right_high) + (dot(left_low, right_high) + dot(left_high, right_low))


def power(base, exponent):
    result = None
    while exponent:
        if exponent & 1:
            result = base if result is None else result * base
        exponent >>= 1
        if exponent:
            base = base * base
    return result


def roots(shift):
    width = jnp.sqrt(shift + 0.25 * shift * shift)
    inverse = 1.0 + 0.5 * shift + width
    return 1.0 / inverse, inverse, width


def radius_column(radii, layers):
    position = lax.broadcasted_iota(jnp.int32, (layers, 1), 0)
    column = jnp.zeros((layers, 1), jnp.float32)
    for mode in range(layers):
        column = jnp.where(position == mode, radii[mode], column)
    return column


def spread_matrix(matrix, count, gather):
    size = matrix.shape[0]
    whole = size * count
    row = lax.broadcasted_iota(jnp.int32, (whole, size), 0)
    item = lax.broadcasted_iota(jnp.int32, (whole, size), 1)
    row_item = row % size if gather else row // count
    left = (row_item == item).astype(jnp.bfloat16)
    column = lax.broadcasted_iota(jnp.int32, (size, whole), 1)
    item = lax.broadcasted_iota(jnp.int32, (size, whole), 0)
    column_item = column // count if gather else column % size
    right = (column_item == item).astype(jnp.bfloat16)
    row = lax.broadcasted_iota(jnp.int32, (whole, whole), 0)
    column = lax.broadcasted_iota(jnp.int32, (whole, whole), 1)
    if gather:
        same = row // size == column % count
    else:
        same = row % count == column // size
    parts = []
    for part in halves(matrix):
        full = dot(dot(left, part).astype(jnp.bfloat16), right)
        parts.append(jnp.where(same, full, 0.0).astype(jnp.bfloat16))
    return tuple(parts)


def forward_kernel(
    sizes, vortex, to_mode, radii, eigen, sine_high, sine_low,
    field, carried, vortex_edge,
    edge, moments, gathered, solved, landed, edge_landed,
    send_a, recv_a, send_b, recv_b, send_e, recv_e,
):
    groups, tiles, layers, rows, width, piece = sizes
    count = groups * tiles
    per_mode = width // piece
    me = lax.axis_index("group") * tiles + lax.axis_index("tile")

    def place(index):
        return (index // tiles, index % tiles)

    barrier = pltpu.get_barrier_semaphore()

    @pl.loop(1, count)
    def _(step):
        pl.semaphore_signal(
            barrier, inc=1, device_id=place((me + step) % count), device_id_type=MESH
        )

    edge[0] = vortex[:, rows - 1, :]
    edge[1] = vortex[:, 0, :]
    pl.semaphore_wait(barrier, count - 1)

    def edge_copy(side):
        target = (me + 1) % count if side == 0 else (me + count - 1) % count
        return pltpu.make_async_remote_copy(
            src_ref=edge.at[side], dst_ref=edge_landed.at[side],
            send_sem=send_e.at[side], recv_sem=recv_e.at[side],
            device_id=place(target), device_id_type=MESH,
        )

    edge_copy(0).start()
    edge_copy(1).start()

    chunk = min(rows, 16)
    mixer = spread_matrix(to_mode[...], chunk, True)
    shift = radius_column(radii, layers) + eigen[...]
    rho, _, _ = roots(shift)
    for part in range(rows // chunk):
        block = vortex[:, part * chunk : (part + 1) * chunk, :].reshape(layers * chunk, width)
        modal = halves(dot3(mixer, halves(block)))
        spectrum = dot3(modal, (sine_high[...], sine_low[...]))
        field[part * chunk : (part + 1) * chunk] = spectrum.reshape(chunk, layers, width)

    ahead = field[0]
    for y in range(1, rows):
        ahead = ahead * rho + field[y]
    behind = field[rows - 1] * rho
    for y in range(rows - 2, -1, -1):
        behind = (behind + field[y]) * rho
    for mode in range(layers):
        for part in range(per_mode):
            span = slice(part * piece, (part + 1) * piece)
            moments[mode * per_mode + part, 0:1, :] = ahead[mode : mode + 1, span]
            moments[mode * per_mode + part, 1:2, :] = behind[mode : mode + 1, span]

    def exchange(source, target, send, recv, step):
        other = (me + step) % count
        return pltpu.make_async_remote_copy(
            src_ref=source.at[other], dst_ref=target.at[me],
            send_sem=send.at[step], recv_sem=recv.at[step],
            device_id=place(other), device_id_type=MESH,
        )

    @pl.loop(1, count)
    def _(step):
        exchange(moments, gathered, send_a, recv_a, step).start()

    gathered[me] = moments[me]
    mine = eigen[0:1, 0:piece]
    for part in range(1, per_mode):
        mine = jnp.where(me % per_mode == part, eigen[0:1, part * piece : (part + 1) * piece], mine)
    own, _, _ = roots(mine + radii[me // per_mode])
    stride = power(own, rows)
    whole = power(own, count * rows + 1)
    scale = 1.0 / (1.0 - whole * whole)

    @pl.loop(1, count)
    def _(step):
        exchange(moments, gathered, send_a, recv_a, step).wait_recv()

    total_ahead = gathered[0, 0:1, :]
    for p in range(1, count):
        total_ahead = total_ahead * stride + gathered[p, 0:1, :]
    total_ahead = total_ahead * own
    total_behind = gathered[count - 1, 1:2, :]
    for p in range(count - 2, -1, -1):
        total_behind = total_behind * stride + gathered[p, 1:2, :]
    first = (total_ahead * whole - total_behind) * scale
    last = (total_behind * whole - total_ahead) * scale * own
    for p in range(count):
        solved[p, 0:1, :] = first
        first = first * stride + gathered[p, 0:1, :]
    for p in range(count - 1, -1, -1):
        solved[p, 1:2, :] = last
        last = last * stride + gathered[p, 1:2, :]

    @pl.loop(1, count)
    def _(step):
        exchange(solved, landed, send_b, recv_b, step).start()

    landed[me] = solved[me]
    edge_copy(0).wait()
    edge_copy(1).wait()
    vortex_edge[0] = jnp.where(me == 0, 0.0, edge_landed[0])
    vortex_edge[1] = jnp.where(me == count - 1, 0.0, edge_landed[1])

    @pl.loop(1, count)
    def _(step):
        exchange(solved, landed, send_b, recv_b, step).wait_recv()

    for mode in range(layers):
        for part in range(per_mode):
            span = slice(part * piece, (part + 1) * piece)
            carried[0, mode : mode + 1, span] = landed[mode * per_mode + part, 0:1, :]
            carried[1, mode : mode + 1, span] = landed[mode * per_mode + part, 1:2, :]

    @pl.loop(1, count)
    def _(step):
        exchange(moments, gathered, send_a, recv_a, step).wait_send()
        exchange(solved, landed, send_b, recv_b, step).wait_send()


def backward_kernel(
    sizes, field, carried, vortex_edge, vortex, wind, mask, to_layer, radii, eigen,
    sine_high, sine_low,
    fresh, stream,
    high, low, stream_pad, vortex_pad, turn, cross,
):
    groups, tiles, layers, rows, width, piece = sizes
    count = groups * tiles
    me = lax.axis_index("group") * tiles + lax.axis_index("tile")
    shift = radius_column(radii, layers) + eigen[...]
    rho, inverse, spread = roots(shift)
    factor = -0.5 / spread

    def keep(slot, value):
        upper, lower = halves(value * factor)
        high[slot * layers : (slot + 1) * layers, :] = upper
        low[slot * layers : (slot + 1) * layers, :] = lower

    ahead = carried[0]
    for y in range(rows):
        ahead = ahead * rho + field[y]
        turn[y] = ahead
    behind = carried[1]
    keep(rows + 1, jnp.where(me == count - 1, 0.0, ahead * rho + behind * inverse))
    for y in range(rows - 1, -1, -1):
        keep(y, turn[y] + behind)
        behind = (behind + field[y]) * rho
    keep(rows, jnp.where(me == 0, 0.0, carried[0] + behind))

    chunk = min(rows, 16)
    top = 8
    sine = (sine_high[...], sine_low[...])
    mixer = spread_matrix(to_layer[...], chunk, False)
    for part in range(rows // chunk):
        span = slice(part * chunk * layers, (part + 1) * chunk * layers)
        modes = dot3((high[span, :], low[span, :]), sine)
        mixed = dot3(mixer, halves(modes)).reshape(layers, chunk, width)
        stream[:, part * chunk : (part + 1) * chunk, :] = mixed
        stream_pad[:, top + part * chunk : top + (part + 1) * chunk, :] = mixed
    span = slice(rows * layers, (rows + 2) * layers)
    modes = dot3((high[span, :], low[span, :]), sine)
    plain = halves(to_layer[...])
    stream_pad[:, top - 1, :] = dot3(plain, halves(modes[:layers]))
    stream_pad[:, top + rows, :] = dot3(plain, halves(modes[layers:]))
    vortex_pad[:, top : top + rows, :] = vortex[...]
    vortex_pad[:, top - 1, :] = vortex_edge[0]
    vortex_pad[:, top + rows, :] = vortex_edge[1]

    deep = rows + 2 * top
    lane = lax.broadcasted_iota(jnp.int32, (deep, width), 1)

    def east_west(value):
        lanes = lane[: value.shape[0]]
        east = jnp.where(lanes == width - 1, 0.0, pltpu.roll(value, width - 1, 1))
        west = jnp.where(lanes == 0, 0.0, pltpu.roll(value, 1, 1))
        return east, west

    middle = slice(top, top + rows)
    north = slice(top + 1, top + rows + 1)
    south = slice(top - 1, top + rows - 1)
    damp = mask[...].astype(jnp.float32) * time_step

    @pl.loop(0, layers)
    def _(layer):
        s_all = stream_pad[layer]
        q_all = vortex_pad[layer]
        s_east, s_west = east_west(s_all)
        q_east, q_west = east_west(q_all)
        s_across = s_east - s_west
        q_across = q_east - q_west
        cross[...] = q_all * s_across - s_all * q_across
        s_mid, q_mid = s_all[middle], q_all[middle]
        s_north, s_south = stream_pad[layer, north, :], stream_pad[layer, south, :]
        s_up = s_north - s_south
        q_up = vortex_pad[layer, north, :] - vortex_pad[layer, south, :]
        p_east, p_west = east_west(s_mid * q_up - q_mid * s_up)
        across = s_across[middle]
        jacobian = (
            across * q_up
            - s_up * q_across[middle]
            + (p_east - p_west)
            + (cross[north, :] - cross[south, :])
        ) * (1.0 / 12.0)
        tendency = -jacobian - (beta_plane * 0.5) * across
        forcing = jnp.where(layer == 0, wind[...], 0.0)
        laplace = s_north + s_south + s_east[middle] + s_west[middle] - 4.0 * s_mid
        drag = jnp.where(layer == layers - 1, bottom_drag, 0.0)
        fresh[layer] = q_mid + damp * (tendency + forcing - drag * laplace)


def body(groups, tiles, vorticity, layer_to_mode, mode_to_layer, inverse_radii, wind, mask):
    layers, rows, width = vorticity.shape
    count = groups * tiles
    piece = layers * width // count
    sizes = (groups, tiles, layers, rows, width, piece)
    sine_high, sine_low = (jnp.asarray(part) for part in sine_parts(width))
    eigen = jnp.asarray(eigen_values(width)[None])
    limit = 56 * 1024 * 1024
    f32, bf16 = jnp.float32, jnp.bfloat16
    dma = pltpu.SemaphoreType.DMA
    field, carried, vortex_edge = pl.pallas_call(
        functools.partial(forward_kernel, sizes),
        out_shape=(
            jax.ShapeDtypeStruct((rows, layers, width), f32),
            jax.ShapeDtypeStruct((2, layers, width), f32),
            jax.ShapeDtypeStruct((2, layers, width), f32),
        ),
        in_specs=[VMEM, VMEM, SMEM, VMEM, VMEM, VMEM],
        out_specs=(VMEM, VMEM, VMEM),
        scratch_shapes=[
            pltpu.VMEM((2, layers, width), f32),
            pltpu.VMEM((count, 2, piece), f32),
            pltpu.VMEM((count, 2, piece), f32),
            pltpu.VMEM((count, 2, piece), f32),
            pltpu.VMEM((count, 2, piece), f32),
            pltpu.VMEM((2, layers, width), f32),
            dma((count,)), dma((count,)), dma((count,)), dma((count,)), dma((2,)), dma((2,)),
        ],
        compiler_params=pltpu.CompilerParams(
            collective_id=0, has_side_effects=True, vmem_limit_bytes=limit
        ),
        name="forward",
    )(vorticity, layer_to_mode, inverse_radii, eigen, sine_high, sine_low)
    total = (rows + 2) * layers
    return pl.pallas_call(
        functools.partial(backward_kernel, sizes),
        out_shape=(
            jax.ShapeDtypeStruct((layers, rows, width), f32),
            jax.ShapeDtypeStruct((layers, rows, width), f32),
        ),
        in_specs=[VMEM] * 7 + [SMEM] + [VMEM] * 3,
        out_specs=(VMEM, VMEM),
        scratch_shapes=[
            pltpu.VMEM((total, width), bf16),
            pltpu.VMEM((total, width), bf16),
            pltpu.VMEM((layers, rows + 16, width), f32),
            pltpu.VMEM((layers, rows + 16, width), f32),
            pltpu.VMEM((rows, layers, width), f32),
            pltpu.VMEM((rows + 16, width), f32),
        ],
        compiler_params=pltpu.CompilerParams(vmem_limit_bytes=limit),
        name="backward",
    )(
        field, carried, vortex_edge, vorticity, wind, mask, mode_to_layer, inverse_radii,
        eigen, sine_high, sine_low,
    )


def solution(mesh):
    groups, tiles = mesh.shape["group"], mesh.shape["tile"]
    rows = P(None, ("group", "tile"), None)
    plane = P(("group", "tile"), None)
    return jax.shard_map(
        functools.partial(body, groups, tiles),
        mesh=mesh,
        in_specs=(rows, P(), P(), P(), plane, plane),
        out_specs=(rows, rows),
        check_vma=False,
    )
```

```python
import functools
import math

import jax
import jax.numpy as jnp
import ml_dtypes
import numpy as np
from jax import lax
from jax.experimental import pallas as pl
from jax.experimental.pallas import tpu as pltpu
from jax.sharding import PartitionSpec as P

time_step = 0.5
beta_plane = 1.0
bottom_drag = 0.2
MESH = pl.DeviceIdType.MESH
ANY = pl.BlockSpec(memory_space=pl.ANY)
VMEM = pl.BlockSpec(memory_space=pltpu.VMEM)
SMEM = pl.BlockSpec(memory_space=pltpu.SMEM)


def sine_parts(length):
    wave = np.arange(length, dtype=np.int64) + 1
    phase = (wave[:, None] * wave[None, :]) % (2 * (length + 1))
    table = math.sqrt(2.0 / (length + 1)) * np.sin(math.pi * phase / (length + 1))
    high = table.astype(np.float32).astype(ml_dtypes.bfloat16)
    low = (table - high.astype(np.float64)).astype(np.float32).astype(ml_dtypes.bfloat16)
    return high, low


def eigen_values(length):
    wave = np.arange(length, dtype=np.float64) + 1
    return (4.0 * np.sin(math.pi * wave / (2 * (length + 1))) ** 2).astype(np.float32)


def halves(value):
    high = value.astype(jnp.bfloat16)
    low = (value - high.astype(jnp.float32)).astype(jnp.bfloat16)
    return high, low


def dot(left, right):
    return jnp.dot(left, right, preferred_element_type=jnp.float32)


def dot3(left, right):
    (left_high, left_low), (right_high, right_low) = left, right
    return dot(left_high, right_high) + (dot(left_low, right_high) + dot(left_high, right_low))


def power(base, exponent):
    result = None
    while exponent:
        if exponent & 1:
            result = base if result is None else result * base
        exponent >>= 1
        if exponent:
            base = base * base
    return result


def roots(shift):
    width = jnp.sqrt(shift + 0.25 * shift * shift)
    inverse = 1.0 + 0.5 * shift + width
    return 1.0 / inverse, inverse, width


def radius_column(radii, layers):
    position = lax.broadcasted_iota(jnp.int32, (layers, 1), 0)
    column = jnp.zeros((layers, 1), jnp.float32)
    for mode in range(layers):
        column = jnp.where(position == mode, radii[mode], column)
    return column


def spread_matrix(matrix, count, gather):
    size = matrix.shape[0]
    whole = size * count
    row = lax.broadcasted_iota(jnp.int32, (whole, size), 0)
    item = lax.broadcasted_iota(jnp.int32, (whole, size), 1)
    row_item = row % size if gather else row // count
    left = (row_item == item).astype(jnp.bfloat16)
    column = lax.broadcasted_iota(jnp.int32, (size, whole), 1)
    item = lax.broadcasted_iota(jnp.int32, (size, whole), 0)
    column_item = column // count if gather else column % size
    right = (column_item == item).astype(jnp.bfloat16)
    row = lax.broadcasted_iota(jnp.int32, (whole, whole), 0)
    column = lax.broadcasted_iota(jnp.int32, (whole, whole), 1)
    if gather:
        same = row // size == column % count
    else:
        same = row % count == column // size
    parts = []
    for part in halves(matrix):
        full = dot(dot(left, part).astype(jnp.bfloat16), right)
        parts.append(jnp.where(same, full, 0.0).astype(jnp.bfloat16))
    return tuple(parts)


def forward_kernel(
    sizes, vortex_in, to_mode, radii, eigen, sine_high_in, sine_low_in,
    field_out, carried, vortex_edge,
    vortex, sine_high, sine_low, field, high, low, local,
    edge, moments, gathered, solved, landed, edge_landed,
    send_a, recv_a, send_b, recv_b, send_e, recv_e,
):
    groups, tiles, layers, rows, width, piece = sizes
    count = groups * tiles
    per_mode = width // piece
    me = lax.axis_index("group") * tiles + lax.axis_index("tile")

    def place(index):
        return (index // tiles, index % tiles)

    loads = [
        pltpu.make_async_copy(vortex_in, vortex, local.at[0]),
        pltpu.make_async_copy(sine_high_in, sine_high, local.at[1]),
        pltpu.make_async_copy(sine_low_in, sine_low, local.at[2]),
    ]
    for load in loads:
        load.start()
    barrier = pltpu.get_barrier_semaphore()

    @pl.loop(1, count)
    def _(step):
        pl.semaphore_signal(
            barrier, inc=1, device_id=place((me + step) % count), device_id_type=MESH
        )

    def edge_copy(side):
        target = (me + 1) % count if side == 0 else (me + count - 1) % count
        return pltpu.make_async_remote_copy(
            src_ref=edge.at[side], dst_ref=edge_landed.at[side],
            send_sem=send_e.at[side], recv_sem=recv_e.at[side],
            device_id=place(target), device_id_type=MESH,
        )

    chunk = min(rows, 16)
    mixer = spread_matrix(to_mode[...], chunk, True)
    shift = radius_column(radii, layers) + eigen[...]
    rho, _, _ = roots(shift)
    loads[0].wait()
    edge[0] = vortex[:, rows - 1, :]
    edge[1] = vortex[:, 0, :]
    for part in range(rows // chunk):
        block = vortex[:, part * chunk : (part + 1) * chunk, :].reshape(layers * chunk, width)
        span = slice(part * chunk * layers, (part + 1) * chunk * layers)
        high[span, :], low[span, :] = halves(dot3(mixer, halves(block)))
    loads[1].wait()
    loads[2].wait()

    def exchange(source, target, send, recv, step):
        other = (me + step) % count
        return pltpu.make_async_remote_copy(
            src_ref=source.at[other], dst_ref=target.at[me],
            send_sem=send.at[step], recv_sem=recv.at[step],
            device_id=place(other), device_id_type=MESH,
        )

    for part in range(per_mode):
        span = slice(part * piece, (part + 1) * piece)
        spectrum = dot3((high[...], low[...]), (sine_high[:, span], sine_low[:, span]))
        field[:, :, span] = spectrum.reshape(rows, layers, piece)
        decay = rho[:, span]
        ahead = field[0, :, span]
        for y in range(1, rows):
            ahead = ahead * decay + field[y, :, span]
        behind = field[rows - 1, :, span] * decay
        for y in range(rows - 2, -1, -1):
            behind = (behind + field[y, :, span]) * decay
        for mode in range(layers):
            moments[mode * per_mode + part, 0:1, :] = ahead[mode : mode + 1]
            moments[mode * per_mode + part, 1:2, :] = behind[mode : mode + 1]
        if part == 0:
            pl.semaphore_wait(barrier, count - 1)

        @pl.loop(0, layers)
        def _(turn):
            other = (me // per_mode + turn) % layers * per_mode + part
            step = (other - me + count) % count

            @pl.when(step != 0)
            def _():
                exchange(moments, gathered, send_a, recv_a, step).start()

    edge_copy(0).start()
    edge_copy(1).start()
    save = pltpu.make_async_copy(field, field_out, local.at[0])
    save.start()
    gathered[me] = moments[me]
    mine = eigen[0:1, 0:piece]
    for part in range(1, per_mode):
        mine = jnp.where(me % per_mode == part, eigen[0:1, part * piece : (part + 1) * piece], mine)
    own, _, _ = roots(mine + radii[me // per_mode])
    stride = power(own, rows)
    whole = power(own, count * rows + 1)
    scale = 1.0 / (1.0 - whole * whole)

    @pl.loop(1, count)
    def _(step):
        exchange(moments, gathered, send_a, recv_a, step).wait_recv()

    total_ahead = gathered[0, 0:1, :]
    for p in range(1, count):
        total_ahead = total_ahead * stride + gathered[p, 0:1, :]
    total_ahead = total_ahead * own
    total_behind = gathered[count - 1, 1:2, :]
    for p in range(count - 2, -1, -1):
        total_behind = total_behind * stride + gathered[p, 1:2, :]
    first = (total_ahead * whole - total_behind) * scale
    last = (total_behind * whole - total_ahead) * scale * own
    for p in range(count):
        solved[p, 0:1, :] = first
        first = first * stride + gathered[p, 0:1, :]
    for p in range(count - 1, -1, -1):
        solved[p, 1:2, :] = last
        last = last * stride + gathered[p, 1:2, :]

    @pl.loop(1, count)
    def _(step):
        exchange(solved, landed, send_b, recv_b, step).start()

    landed[me] = solved[me]
    edge_copy(0).wait()
    edge_copy(1).wait()
    vortex_edge[0] = jnp.where(me == 0, 0.0, edge_landed[0])
    vortex_edge[1] = jnp.where(me == count - 1, 0.0, edge_landed[1])

    @pl.loop(1, count)
    def _(step):
        exchange(solved, landed, send_b, recv_b, step).wait_recv()

    for mode in range(layers):
        for part in range(per_mode):
            span = slice(part * piece, (part + 1) * piece)
            carried[0, mode : mode + 1, span] = landed[mode * per_mode + part, 0:1, :]
            carried[1, mode : mode + 1, span] = landed[mode * per_mode + part, 1:2, :]

    @pl.loop(1, count)
    def _(step):
        exchange(moments, gathered, send_a, recv_a, step).wait_send()
        exchange(solved, landed, send_b, recv_b, step).wait_send()

    save.wait()


def backward_kernel(
    sizes, field, carried, vortex_edge, vortex, wind, mask, to_layer, radii, eigen,
    sine_high_in, sine_low_in,
    fresh_out, stream,
    high, low, stream_pad, vortex_pad, turn, cross, cross_edge,
    sine_high, sine_low, fresh, local, sent, saved,
):
    groups, tiles, layers, rows, width, piece = sizes
    count = groups * tiles
    me = lax.axis_index("group") * tiles + lax.axis_index("tile")
    top = 8
    loads = [
        pltpu.make_async_copy(sine_high_in, sine_high, local.at[0]),
        pltpu.make_async_copy(sine_low_in, sine_low, local.at[1]),
        pltpu.make_async_copy(vortex, vortex_pad.at[:, pl.ds(top, rows), :], local.at[2]),
    ]
    for load in loads:
        load.start()
    shift = radius_column(radii, layers) + eigen[...]
    rho, inverse, spread = roots(shift)
    factor = -0.5 / spread

    def keep(slot, value):
        upper, lower = halves(value * factor)
        high[slot * layers : (slot + 1) * layers, :] = upper
        low[slot * layers : (slot + 1) * layers, :] = lower

    ahead = carried[0]
    for y in range(rows):
        ahead = ahead * rho + field[y]
        turn[y] = ahead
    behind = carried[1]
    keep(rows + 1, jnp.where(me == count - 1, 0.0, ahead * rho + behind * inverse))
    for y in range(rows - 1, -1, -1):
        keep(y, turn[y] + behind)
        behind = (behind + field[y]) * rho
    keep(rows, jnp.where(me == 0, 0.0, carried[0] + behind))

    chunk = min(rows, 16)
    loads[0].wait()
    loads[1].wait()
    sine = (sine_high[...], sine_low[...])
    mixer = spread_matrix(to_layer[...], chunk, False)

    def store(part):
        return pltpu.make_async_copy(
            stream_pad.at[:, pl.ds(top + part * chunk, chunk), :],
            stream.at[:, pl.ds(part * chunk, chunk), :],
            sent.at[part],
        )

    for part in range(rows // chunk):
        span = slice(part * chunk * layers, (part + 1) * chunk * layers)
        modes = dot3((high[span, :], low[span, :]), sine)
        mixed = dot3(mixer, halves(modes)).reshape(layers, chunk, width)
        stream_pad[:, top + part * chunk : top + (part + 1) * chunk, :] = mixed
        store(part).start()
    span = slice(rows * layers, (rows + 2) * layers)
    modes = dot3((high[span, :], low[span, :]), sine)
    plain = halves(to_layer[...])
    lane = lax.broadcasted_iota(jnp.int32, (max(rows, layers), width), 1)

    def east_west(value):
        lanes = lane[: value.shape[0]]
        east = jnp.where(lanes == width - 1, 0.0, pltpu.roll(value, width - 1, 1))
        west = jnp.where(lanes == 0, 0.0, pltpu.roll(value, 1, 1))
        return east, west

    for side, row in ((0, top - 1), (1, top + rows)):
        s_edge = dot3(plain, halves(modes[side * layers : (side + 1) * layers]))
        q_edge = vortex_edge[side]
        s_east, s_west = east_west(s_edge)
        q_east, q_west = east_west(q_edge)
        cross_edge[side] = q_edge * (s_east - s_west) - s_edge * (q_east - q_west)
        stream_pad[:, row, :] = s_edge
        vortex_pad[:, row, :] = q_edge
    loads[2].wait()

    middle = slice(top, top + rows)
    north = slice(top + 1, top + rows + 1)
    south = slice(top - 1, top + rows - 1)

    def finish(layer):
        return pltpu.make_async_copy(fresh.at[layer], fresh_out.at[layer], saved.at[layer])

    damp = mask[...].astype(jnp.float32) * time_step

    @pl.loop(0, layers)
    def _(layer):
        s_mid = stream_pad[layer, middle, :]
        q_mid = vortex_pad[layer, middle, :]
        s_east, s_west = east_west(s_mid)
        q_east, q_west = east_west(q_mid)
        s_across = s_east - s_west
        q_across = q_east - q_west
        cross[middle, :] = q_mid * s_across - s_mid * q_across
        cross[top - 1 : top, :] = cross_edge[0, pl.ds(layer, 1), :]
        cross[top + rows : top + rows + 1, :] = cross_edge[1, pl.ds(layer, 1), :]
        s_north, s_south = stream_pad[layer, north, :], stream_pad[layer, south, :]
        s_up = s_north - s_south
        q_up = vortex_pad[layer, north, :] - vortex_pad[layer, south, :]
        p_east, p_west = east_west(s_mid * q_up - q_mid * s_up)
        jacobian = (
            s_across * q_up
            - s_up * q_across
            + (p_east - p_west)
            + (cross[north, :] - cross[south, :])
        ) * (1.0 / 12.0)
        tendency = -jacobian - (beta_plane * 0.5) * s_across
        forcing = jnp.where(layer == 0, wind[...], 0.0)
        laplace = s_north + s_south + s_east + s_west - 4.0 * s_mid
        drag = jnp.where(layer == layers - 1, bottom_drag, 0.0)
        fresh[layer] = q_mid + damp * (tendency + forcing - drag * laplace)
        finish(layer).start()

    @pl.loop(0, layers)
    def _(layer):
        finish(layer).wait()

    for part in range(rows // chunk):
        store(part).wait()


def body(groups, tiles, vorticity, layer_to_mode, mode_to_layer, inverse_radii, wind, mask):
    layers, rows, width = vorticity.shape
    count = groups * tiles
    piece = layers * width // count
    sizes = (groups, tiles, layers, rows, width, piece)
    sine_high, sine_low = (jnp.asarray(part) for part in sine_parts(width))
    eigen = jnp.asarray(eigen_values(width)[None])
    limit = 56 * 1024 * 1024
    f32, bf16 = jnp.float32, jnp.bfloat16
    dma = pltpu.SemaphoreType.DMA
    field, carried, vortex_edge = pl.pallas_call(
        functools.partial(forward_kernel, sizes),
        out_shape=(
            jax.ShapeDtypeStruct((rows, layers, width), f32),
            jax.ShapeDtypeStruct((2, layers, width), f32),
            jax.ShapeDtypeStruct((2, layers, width), f32),
        ),
        in_specs=[ANY, VMEM, SMEM, VMEM, ANY, ANY],
        out_specs=(ANY, VMEM, VMEM),
        scratch_shapes=[
            pltpu.VMEM((layers, rows, width), f32),
            pltpu.VMEM((width, width), bf16),
            pltpu.VMEM((width, width), bf16),
            pltpu.VMEM((rows, layers, width), f32),
            pltpu.VMEM((rows * layers, width), bf16),
            pltpu.VMEM((rows * layers, width), bf16),
            dma((3,)),
            pltpu.VMEM((2, layers, width), f32),
            pltpu.VMEM((count, 2, piece), f32),
            pltpu.VMEM((count, 2, piece), f32),
            pltpu.VMEM((count, 2, piece), f32),
            pltpu.VMEM((count, 2, piece), f32),
            pltpu.VMEM((2, layers, width), f32),
            dma((count,)), dma((count,)), dma((count,)), dma((count,)), dma((2,)), dma((2,)),
        ],
        compiler_params=pltpu.CompilerParams(
            collective_id=0, has_side_effects=True, vmem_limit_bytes=limit
        ),
        name="forward",
    )(vorticity, layer_to_mode, inverse_radii, eigen, sine_high, sine_low)
    total = (rows + 2) * layers
    return pl.pallas_call(
        functools.partial(backward_kernel, sizes),
        out_shape=(
            jax.ShapeDtypeStruct((layers, rows, width), f32),
            jax.ShapeDtypeStruct((layers, rows, width), f32),
        ),
        in_specs=[VMEM] * 3 + [ANY] + [VMEM] * 3 + [SMEM, VMEM, ANY, ANY],
        out_specs=(ANY, ANY),
        scratch_shapes=[
            pltpu.VMEM((total, width), bf16),
            pltpu.VMEM((total, width), bf16),
            pltpu.VMEM((layers, rows + 16, width), f32),
            pltpu.VMEM((layers, rows + 16, width), f32),
            pltpu.VMEM((rows, layers, width), f32),
            pltpu.VMEM((rows + 16, width), f32),
            pltpu.VMEM((2, layers, width), f32),
            pltpu.VMEM((width, width), bf16),
            pltpu.VMEM((width, width), bf16),
            pltpu.VMEM((layers, rows, width), f32),
            dma((3,)), dma((rows // min(rows, 16),)), dma((layers,)),
        ],
        compiler_params=pltpu.CompilerParams(vmem_limit_bytes=limit),
        name="backward",
    )(
        field, carried, vortex_edge, vorticity, wind, mask, mode_to_layer, inverse_radii,
        eigen, sine_high, sine_low,
    )


def solution(mesh):
    groups, tiles = mesh.shape["group"], mesh.shape["tile"]
    rows = P(None, ("group", "tile"), None)
    plane = P(("group", "tile"), None)
    return jax.shard_map(
        functools.partial(body, groups, tiles),
        mesh=mesh,
        in_specs=(rows, P(), P(), P(), plane, plane),
        out_specs=(rows, rows),
        check_vma=False,
    )
```

```python
import functools
import math

import jax
import jax.numpy as jnp
import ml_dtypes
import numpy as np
from jax import lax
from jax.experimental import pallas as pl
from jax.experimental.pallas import tpu as pltpu
from jax.sharding import PartitionSpec as P

time_step = 0.5
beta_plane = 1.0
bottom_drag = 0.2
MESH = pl.DeviceIdType.MESH
ANY = pl.BlockSpec(memory_space=pl.ANY)
VMEM = pl.BlockSpec(memory_space=pltpu.VMEM)
SMEM = pl.BlockSpec(memory_space=pltpu.SMEM)


def sine_parts(length):
    wave = np.arange(length, dtype=np.int64) + 1
    phase = (wave[:, None] * wave[None, :]) % (2 * (length + 1))
    table = math.sqrt(2.0 / (length + 1)) * np.sin(math.pi * phase / (length + 1))
    high = table.astype(np.float32).astype(ml_dtypes.bfloat16)
    low = (table - high.astype(np.float64)).astype(np.float32).astype(ml_dtypes.bfloat16)
    return high, low


def eigen_values(length):
    wave = np.arange(length, dtype=np.float64) + 1
    return (4.0 * np.sin(math.pi * wave / (2 * (length + 1))) ** 2).astype(np.float32)


def halves(value):
    high = value.astype(jnp.bfloat16)
    low = (value - high.astype(jnp.float32)).astype(jnp.bfloat16)
    return high, low


def dot(left, right):
    return jnp.dot(left, right, preferred_element_type=jnp.float32)


def dot3(left, right):
    (left_high, left_low), (right_high, right_low) = left, right
    return dot(left_high, right_high) + (dot(left_low, right_high) + dot(left_high, right_low))


def power(base, exponent):
    result = None
    while exponent:
        if exponent & 1:
            result = base if result is None else result * base
        exponent >>= 1
        if exponent:
            base = base * base
    return result


def roots(shift):
    width = jnp.sqrt(shift + 0.25 * shift * shift)
    inverse = 1.0 + 0.5 * shift + width
    return 1.0 / inverse, inverse, width


def radius_column(radii, layers):
    position = lax.broadcasted_iota(jnp.int32, (layers, 1), 0)
    column = jnp.zeros((layers, 1), jnp.float32)
    for mode in range(layers):
        column = jnp.where(position == mode, radii[mode], column)
    return column


def spread_matrix(matrix, count, gather):
    size = matrix.shape[0]
    whole = size * count
    row = lax.broadcasted_iota(jnp.int32, (whole, size), 0)
    item = lax.broadcasted_iota(jnp.int32, (whole, size), 1)
    row_item = row % size if gather else row // count
    left = (row_item == item).astype(jnp.bfloat16)
    column = lax.broadcasted_iota(jnp.int32, (size, whole), 1)
    item = lax.broadcasted_iota(jnp.int32, (size, whole), 0)
    column_item = column // count if gather else column % size
    right = (column_item == item).astype(jnp.bfloat16)
    row = lax.broadcasted_iota(jnp.int32, (whole, whole), 0)
    column = lax.broadcasted_iota(jnp.int32, (whole, whole), 1)
    if gather:
        same = row // size == column % count
    else:
        same = row % count == column // size
    parts = []
    for part in halves(matrix):
        full = dot(dot(left, part).astype(jnp.bfloat16), right)
        parts.append(jnp.where(same, full, 0.0).astype(jnp.bfloat16))
    return tuple(parts)


def forward_kernel(
    sizes, vortex_in, to_mode, radii, eigen, sine_high_in, sine_low_in,
    field_out, carried, vortex_edge,
    vortex, sine_high, sine_low, field, high, low, local,
    edge, moments, gathered, solved, landed, edge_landed,
    send_a, recv_a, send_b, recv_b, send_e, recv_e,
):
    groups, tiles, layers, rows, width, piece = sizes
    count = groups * tiles
    per_mode = width // piece
    me = lax.axis_index("group") * tiles + lax.axis_index("tile")

    def place(index):
        return (lax.div(index, tiles), lax.rem(index, tiles))

    def wrap(index):
        return jnp.where(index >= count, index - count, index)

    loads = [
        pltpu.make_async_copy(vortex_in, vortex, local.at[0]),
        pltpu.make_async_copy(sine_high_in, sine_high, local.at[1]),
        pltpu.make_async_copy(sine_low_in, sine_low, local.at[2]),
    ]
    for load in loads:
        load.start()
    barrier = pltpu.get_barrier_semaphore()

    @pl.loop(1, count)
    def _(step):
        pl.semaphore_signal(
            barrier, inc=1, device_id=place(wrap(me + step)), device_id_type=MESH
        )

    def edge_copy(side):
        target = (me + 1) % count if side == 0 else (me + count - 1) % count
        return pltpu.make_async_remote_copy(
            src_ref=edge.at[side], dst_ref=edge_landed.at[side],
            send_sem=send_e.at[side], recv_sem=recv_e.at[side],
            device_id=place(target), device_id_type=MESH,
        )

    chunk = min(rows, 16)
    mixer = spread_matrix(to_mode[...], chunk, True)
    shift = radius_column(radii, layers) + eigen[...]
    rho, _, _ = roots(shift)
    loads[0].wait()
    edge[0] = vortex[:, rows - 1, :]
    edge[1] = vortex[:, 0, :]
    for part in range(rows // chunk):
        block = vortex[:, part * chunk : (part + 1) * chunk, :].reshape(layers * chunk, width)
        span = slice(part * chunk * layers, (part + 1) * chunk * layers)
        high[span, :], low[span, :] = halves(dot3(mixer, halves(block)))
    loads[1].wait()
    loads[2].wait()

    def exchange(source, target, send, recv, step):
        other = wrap(me + step)
        return pltpu.make_async_remote_copy(
            src_ref=source.at[other], dst_ref=target.at[me],
            send_sem=send.at[step], recv_sem=recv.at[step],
            device_id=place(other), device_id_type=MESH,
        )

    home = lax.div(me, per_mode)
    for part in range(per_mode):
        span = slice(part * piece, (part + 1) * piece)
        spectrum = dot3((high[...], low[...]), (sine_high[:, span], sine_low[:, span]))
        field[:, :, span] = spectrum.reshape(rows, layers, piece)
        decay = rho[:, span]
        ahead = field[0, :, span]
        for y in range(1, rows):
            ahead = ahead * decay + field[y, :, span]
        behind = field[rows - 1, :, span] * decay
        for y in range(rows - 2, -1, -1):
            behind = (behind + field[y, :, span]) * decay
        for mode in range(layers):
            moments[mode * per_mode + part, 0:1, :] = ahead[mode : mode + 1]
            moments[mode * per_mode + part, 1:2, :] = behind[mode : mode + 1]
        if part == 0:
            pl.semaphore_wait(barrier, count - 1)

        @pl.loop(0, layers)
        def _(turn):
            other = lax.rem(home + turn, layers) * per_mode + part
            step = wrap(other - me + count)

            @pl.when(step != 0)
            def _():
                exchange(moments, gathered, send_a, recv_a, step).start()

    edge_copy(0).start()
    edge_copy(1).start()
    save = pltpu.make_async_copy(field, field_out, local.at[0])
    save.start()
    gathered[me] = moments[me]
    mine = eigen[0:1, 0:piece]
    for part in range(1, per_mode):
        mine = jnp.where(me % per_mode == part, eigen[0:1, part * piece : (part + 1) * piece], mine)
    own, _, _ = roots(mine + radii[me // per_mode])
    stride = power(own, rows)
    whole = power(own, count * rows + 1)
    scale = 1.0 / (1.0 - whole * whole)

    @pl.loop(1, count)
    def _(step):
        exchange(moments, gathered, send_a, recv_a, step).wait_recv()

    total_ahead = gathered[0, 0:1, :]
    for p in range(1, count):
        total_ahead = total_ahead * stride + gathered[p, 0:1, :]
    total_ahead = total_ahead * own
    total_behind = gathered[count - 1, 1:2, :]
    for p in range(count - 2, -1, -1):
        total_behind = total_behind * stride + gathered[p, 1:2, :]
    first = (total_ahead * whole - total_behind) * scale
    last = (total_behind * whole - total_ahead) * scale * own
    for p in range(count):
        solved[p, 0:1, :] = first
        first = first * stride + gathered[p, 0:1, :]
    for p in range(count - 1, -1, -1):
        solved[p, 1:2, :] = last
        last = last * stride + gathered[p, 1:2, :]

    @pl.loop(1, count)
    def _(step):
        exchange(solved, landed, send_b, recv_b, step).start()

    landed[me] = solved[me]
    edge_copy(0).wait()
    edge_copy(1).wait()
    vortex_edge[0] = jnp.where(me == 0, 0.0, edge_landed[0])
    vortex_edge[1] = jnp.where(me == count - 1, 0.0, edge_landed[1])

    @pl.loop(1, count)
    def _(step):
        exchange(solved, landed, send_b, recv_b, step).wait_recv()

    for mode in range(layers):
        for part in range(per_mode):
            span = slice(part * piece, (part + 1) * piece)
            carried[0, mode : mode + 1, span] = landed[mode * per_mode + part, 0:1, :]
            carried[1, mode : mode + 1, span] = landed[mode * per_mode + part, 1:2, :]

    @pl.loop(1, count)
    def _(step):
        exchange(moments, gathered, send_a, recv_a, step).wait_send()
        exchange(solved, landed, send_b, recv_b, step).wait_send()

    save.wait()


def backward_kernel(
    sizes, field, carried, vortex_edge, vortex, wind, mask, to_layer, radii, eigen,
    sine_high_in, sine_low_in,
    fresh_out, stream,
    high, low, stream_pad, vortex_pad, turn, cross, cross_edge,
    sine_high, sine_low, fresh, partial, damp, local, sent, saved,
):
    groups, tiles, layers, rows, width, piece = sizes
    count = groups * tiles
    me = lax.axis_index("group") * tiles + lax.axis_index("tile")
    top = 8
    loads = [
        pltpu.make_async_copy(sine_high_in, sine_high, local.at[0]),
        pltpu.make_async_copy(sine_low_in, sine_low, local.at[1]),
        pltpu.make_async_copy(vortex, vortex_pad.at[:, pl.ds(top, rows), :], local.at[2]),
    ]
    for load in loads:
        load.start()
    shift = radius_column(radii, layers) + eigen[...]
    rho, inverse, spread = roots(shift)
    factor = -0.5 / spread

    def keep(slot, value):
        upper, lower = halves(value * factor)
        high[slot * layers : (slot + 1) * layers, :] = upper
        low[slot * layers : (slot + 1) * layers, :] = lower

    ahead = carried[0]
    for y in range(rows):
        ahead = ahead * rho + field[y]
        turn[y] = ahead
    behind = carried[1]
    keep(rows + 1, jnp.where(me == count - 1, 0.0, ahead * rho + behind * inverse))
    for y in range(rows - 1, -1, -1):
        keep(y, turn[y] + behind)
        behind = (behind + field[y]) * rho
    keep(rows, jnp.where(me == 0, 0.0, carried[0] + behind))

    chunk = min(rows, 16)
    loads[0].wait()
    loads[1].wait()
    sine = (sine_high[...], sine_low[...])
    mixer = spread_matrix(to_layer[...], chunk, False)

    def store(part):
        return pltpu.make_async_copy(
            stream_pad.at[:, pl.ds(top + part * chunk, chunk), :],
            stream.at[:, pl.ds(part * chunk, chunk), :],
            sent.at[part],
        )

    for part in range(rows // chunk):
        span = slice(part * chunk * layers, (part + 1) * chunk * layers)
        modes = dot3((high[span, :], low[span, :]), sine)
        mixed = dot3(mixer, halves(modes)).reshape(layers, chunk, width)
        stream_pad[:, top + part * chunk : top + (part + 1) * chunk, :] = mixed
        store(part).start()
    span = slice(rows * layers, (rows + 2) * layers)
    modes = dot3((high[span, :], low[span, :]), sine)
    plain = halves(to_layer[...])
    lane = lax.broadcasted_iota(jnp.int32, (max(rows, layers), width), 1)

    def east_west(value):
        lanes = lane[: value.shape[0]]
        east = jnp.where(lanes == width - 1, 0.0, pltpu.roll(value, width - 1, 1))
        west = jnp.where(lanes == 0, 0.0, pltpu.roll(value, 1, 1))
        return east, west

    for side, row in ((0, top - 1), (1, top + rows)):
        s_edge = dot3(plain, halves(modes[side * layers : (side + 1) * layers]))
        q_edge = vortex_edge[side]
        s_east, s_west = east_west(s_edge)
        q_east, q_west = east_west(q_edge)
        cross_edge[side] = q_edge * (s_east - s_west) - s_edge * (q_east - q_west)
        stream_pad[:, row, :] = s_edge
        vortex_pad[:, row, :] = q_edge
    loads[2].wait()

    def finish(layer):
        return pltpu.make_async_copy(fresh.at[layer], fresh_out.at[layer], saved.at[layer])

    damp[...] = mask[...].astype(jnp.float32) * time_step

    block = 8

    @pl.loop(0, layers)
    def _(layer):
        cross[top - 1 : top, :] = cross_edge[0, pl.ds(layer, 1), :]
        cross[top + rows : top + rows + 1, :] = cross_edge[1, pl.ds(layer, 1), :]
        for start in range(top, top + rows, block):
            here = slice(start, start + block)
            north, south = slice(start + 1, start + block + 1), slice(start - 1, start + block - 1)
            s_mid, q_mid = stream_pad[layer, here, :], vortex_pad[layer, here, :]
            s_east, s_west = east_west(s_mid)
            q_east, q_west = east_west(q_mid)
            s_across = s_east - s_west
            q_across = q_east - q_west
            cross[here, :] = q_mid * s_across - s_mid * q_across
            s_up = stream_pad[layer, north, :] - stream_pad[layer, south, :]
            q_up = vortex_pad[layer, north, :] - vortex_pad[layer, south, :]
            p_east, p_west = east_west(s_mid * q_up - q_mid * s_up)
            partial[start - top : start - top + block, :] = (
                (s_across * q_up - s_up * q_across + (p_east - p_west)) * (1.0 / 12.0)
                + (beta_plane * 0.5) * s_across
            )
        for start in range(top, top + rows, block):
            here = slice(start, start + block)
            north, south = slice(start + 1, start + block + 1), slice(start - 1, start + block - 1)
            out = slice(start - top, start - top + block)
            loss = partial[out, :] + (cross[north, :] - cross[south, :]) * (1.0 / 12.0)
            fresh[layer, out, :] = vortex_pad[layer, here, :] - damp[out, :] * loss

        @pl.when(layer == 0)
        def _():
            fresh[layer] = fresh[layer] + damp[...] * wind[...]

        @pl.when(layer == layers - 1)
        def _():
            s_mid = stream_pad[layer, top : top + rows, :]
            s_east, s_west = east_west(s_mid)
            s_north = stream_pad[layer, top + 1 : top + rows + 1, :]
            s_south = stream_pad[layer, top - 1 : top + rows - 1, :]
            laplace = s_north + s_south + s_east + s_west - 4.0 * s_mid
            fresh[layer] = fresh[layer] - (bottom_drag * damp[...]) * laplace

        finish(layer).start()

    @pl.loop(0, layers)
    def _(layer):
        finish(layer).wait()

    for part in range(rows // chunk):
        store(part).wait()


def body(groups, tiles, vorticity, layer_to_mode, mode_to_layer, inverse_radii, wind, mask):
    layers, rows, width = vorticity.shape
    count = groups * tiles
    piece = layers * width // count
    sizes = (groups, tiles, layers, rows, width, piece)
    sine_high, sine_low = (jnp.asarray(part) for part in sine_parts(width))
    eigen = jnp.asarray(eigen_values(width)[None])
    limit = 56 * 1024 * 1024
    f32, bf16 = jnp.float32, jnp.bfloat16
    dma = pltpu.SemaphoreType.DMA
    field, carried, vortex_edge = pl.pallas_call(
        functools.partial(forward_kernel, sizes),
        out_shape=(
            jax.ShapeDtypeStruct((rows, layers, width), f32),
            jax.ShapeDtypeStruct((2, layers, width), f32),
            jax.ShapeDtypeStruct((2, layers, width), f32),
        ),
        in_specs=[ANY, VMEM, SMEM, VMEM, ANY, ANY],
        out_specs=(ANY, VMEM, VMEM),
        scratch_shapes=[
            pltpu.VMEM((layers, rows, width), f32),
            pltpu.VMEM((width, width), bf16),
            pltpu.VMEM((width, width), bf16),
            pltpu.VMEM((rows, layers, width), f32),
            pltpu.VMEM((rows * layers, width), bf16),
            pltpu.VMEM((rows * layers, width), bf16),
            dma((3,)),
            pltpu.VMEM((2, layers, width), f32),
            pltpu.VMEM((count, 2, piece), f32),
            pltpu.VMEM((count, 2, piece), f32),
            pltpu.VMEM((count, 2, piece), f32),
            pltpu.VMEM((count, 2, piece), f32),
            pltpu.VMEM((2, layers, width), f32),
            dma((count,)), dma((count,)), dma((count,)), dma((count,)), dma((2,)), dma((2,)),
        ],
        compiler_params=pltpu.CompilerParams(
            collective_id=0, has_side_effects=True, vmem_limit_bytes=limit
        ),
        name="forward",
    )(vorticity, layer_to_mode, inverse_radii, eigen, sine_high, sine_low)
    total = (rows + 2) * layers
    return pl.pallas_call(
        functools.partial(backward_kernel, sizes),
        out_shape=(
            jax.ShapeDtypeStruct((layers, rows, width), f32),
            jax.ShapeDtypeStruct((layers, rows, width), f32),
        ),
        in_specs=[VMEM] * 3 + [ANY] + [VMEM] * 3 + [SMEM, VMEM, ANY, ANY],
        out_specs=(ANY, ANY),
        scratch_shapes=[
            pltpu.VMEM((total, width), bf16),
            pltpu.VMEM((total, width), bf16),
            pltpu.VMEM((layers, rows + 16, width), f32),
            pltpu.VMEM((layers, rows + 16, width), f32),
            pltpu.VMEM((rows, layers, width), f32),
            pltpu.VMEM((rows + 16, width), f32),
            pltpu.VMEM((2, layers, width), f32),
            pltpu.VMEM((width, width), bf16),
            pltpu.VMEM((width, width), bf16),
            pltpu.VMEM((layers, rows, width), f32),
            pltpu.VMEM((rows, width), f32),
            pltpu.VMEM((rows, width), f32),
            dma((3,)), dma((rows // min(rows, 16),)), dma((layers,)),
        ],
        compiler_params=pltpu.CompilerParams(vmem_limit_bytes=limit),
        name="backward",
    )(
        field, carried, vortex_edge, vorticity, wind, mask, mode_to_layer, inverse_radii,
        eigen, sine_high, sine_low,
    )


def solution(mesh):
    groups, tiles = mesh.shape["group"], mesh.shape["tile"]
    rows = P(None, ("group", "tile"), None)
    plane = P(("group", "tile"), None)
    return jax.shard_map(
        functools.partial(body, groups, tiles),
        mesh=mesh,
        in_specs=(rows, P(), P(), P(), plane, plane),
        out_specs=(rows, rows),
        check_vma=False,
    )
```

```python
import functools
import math

import jax
import jax.numpy as jnp
import ml_dtypes
import numpy as np
from jax import lax
from jax.experimental import pallas as pl
from jax.experimental.pallas import tpu as pltpu
from jax.sharding import PartitionSpec as P

time_step = 0.5
beta_plane = 1.0
bottom_drag = 0.2
MESH = pl.DeviceIdType.MESH
ANY = pl.BlockSpec(memory_space=pl.ANY)
VMEM = pl.BlockSpec(memory_space=pltpu.VMEM)
SMEM = pl.BlockSpec(memory_space=pltpu.SMEM)


def sine_parts(length):
    wave = np.arange(length, dtype=np.int64) + 1
    phase = (wave[:, None] * wave[None, :]) % (2 * (length + 1))
    table = math.sqrt(2.0 / (length + 1)) * np.sin(math.pi * phase / (length + 1))
    high = table.astype(np.float32).astype(ml_dtypes.bfloat16)
    low = (table - high.astype(np.float64)).astype(np.float32).astype(ml_dtypes.bfloat16)
    return high, low


def eigen_values(length):
    wave = np.arange(length, dtype=np.float64) + 1
    return (4.0 * np.sin(math.pi * wave / (2 * (length + 1))) ** 2).astype(np.float32)


def halves(value):
    high = value.astype(jnp.bfloat16)
    low = (value - high.astype(jnp.float32)).astype(jnp.bfloat16)
    return high, low


def dot(left, right):
    return jnp.dot(left, right, preferred_element_type=jnp.float32)


def dot3(left, right):
    right_high, right_low = right
    rows = left.shape[0] // 2
    wide = dot(left, right_high)
    return wide[:rows] + (wide[rows:] + dot(left[:rows], right_low))


def power(base, exponent):
    result = None
    while exponent:
        if exponent & 1:
            result = base if result is None else result * base
        exponent >>= 1
        if exponent:
            base = base * base
    return result


def roots(shift):
    width = jnp.sqrt(shift + 0.25 * shift * shift)
    inverse = 1.0 + 0.5 * shift + width
    return 1.0 / inverse, inverse, width


def radius_column(radii, layers):
    position = lax.broadcasted_iota(jnp.int32, (layers, 1), 0)
    column = jnp.zeros((layers, 1), jnp.float32)
    for mode in range(layers):
        column = jnp.where(position == mode, radii[mode], column)
    return column


def spread_matrix(matrix, count, gather):
    size = matrix.shape[0]
    whole = size * count
    row = lax.broadcasted_iota(jnp.int32, (whole, size), 0)
    item = lax.broadcasted_iota(jnp.int32, (whole, size), 1)
    row_item = row % size if gather else row // count
    left = (row_item == item).astype(jnp.bfloat16)
    column = lax.broadcasted_iota(jnp.int32, (size, whole), 1)
    item = lax.broadcasted_iota(jnp.int32, (size, whole), 0)
    column_item = column // count if gather else column % size
    right = (column_item == item).astype(jnp.bfloat16)
    row = lax.broadcasted_iota(jnp.int32, (whole, whole), 0)
    column = lax.broadcasted_iota(jnp.int32, (whole, whole), 1)
    if gather:
        same = row // size == column % count
    else:
        same = row % count == column // size
    parts = []
    for part in halves(matrix):
        full = dot(dot(left, part).astype(jnp.bfloat16), right)
        parts.append(jnp.where(same, full, 0.0).astype(jnp.bfloat16))
    return jnp.concatenate(parts, axis=0)


def forward_kernel(
    sizes, vortex_in, to_mode, radii, eigen, sine_high_in, sine_low_in,
    field_out, carried, vortex_edge,
    vortex, sine_high, sine_low, field, both, local,
    edge, moments, gathered, solved, landed, edge_landed,
    send_a, recv_a, send_b, recv_b, send_e, recv_e,
):
    groups, tiles, layers, rows, width, piece = sizes
    count = groups * tiles
    per_mode = width // piece
    me = lax.axis_index("group") * tiles + lax.axis_index("tile")

    def place(index):
        return (lax.div(index, tiles), lax.rem(index, tiles))

    def wrap(index):
        return jnp.where(index >= count, index - count, index)

    loads = [
        pltpu.make_async_copy(vortex_in, vortex, local.at[0]),
        pltpu.make_async_copy(sine_high_in, sine_high, local.at[1]),
        pltpu.make_async_copy(sine_low_in, sine_low, local.at[2]),
    ]
    for load in loads:
        load.start()
    barrier = pltpu.get_barrier_semaphore()

    @pl.loop(1, count)
    def _(step):
        pl.semaphore_signal(
            barrier, inc=1, device_id=place(wrap(me + step)), device_id_type=MESH
        )

    def edge_copy(side):
        target = (me + 1) % count if side == 0 else (me + count - 1) % count
        return pltpu.make_async_remote_copy(
            src_ref=edge.at[side], dst_ref=edge_landed.at[side],
            send_sem=send_e.at[side], recv_sem=recv_e.at[side],
            device_id=place(target), device_id_type=MESH,
        )

    chunk = min(rows, 16)
    mixer = spread_matrix(to_mode[...], chunk, True)
    shift = radius_column(radii, layers) + eigen[...]
    rho, _, _ = roots(shift)
    loads[0].wait()
    edge[0] = vortex[:, rows - 1, :]
    edge[1] = vortex[:, 0, :]
    for part in range(rows // chunk):
        block = vortex[:, part * chunk : (part + 1) * chunk, :].reshape(layers * chunk, width)
        low_at = rows * layers
        span = slice(part * chunk * layers, (part + 1) * chunk * layers)
        low_span = slice(low_at + part * chunk * layers, low_at + (part + 1) * chunk * layers)
        both[span, :], both[low_span, :] = halves(dot3(mixer, halves(block)))
    loads[1].wait()
    loads[2].wait()

    def exchange(source, target, send, recv, step):
        other = wrap(me + step)
        return pltpu.make_async_remote_copy(
            src_ref=source.at[other], dst_ref=target.at[me],
            send_sem=send.at[step], recv_sem=recv.at[step],
            device_id=place(other), device_id_type=MESH,
        )

    home = lax.div(me, per_mode)
    for part in range(per_mode):
        span = slice(part * piece, (part + 1) * piece)
        spectrum = dot3(both[...], (sine_high[:, span], sine_low[:, span]))
        field[:, :, span] = spectrum.reshape(rows, layers, piece)
        decay = rho[:, span]
        ahead = field[0, :, span]
        for y in range(1, rows):
            ahead = ahead * decay + field[y, :, span]
        behind = field[rows - 1, :, span] * decay
        for y in range(rows - 2, -1, -1):
            behind = (behind + field[y, :, span]) * decay
        for mode in range(layers):
            moments[mode * per_mode + part, 0:1, :] = ahead[mode : mode + 1]
            moments[mode * per_mode + part, 1:2, :] = behind[mode : mode + 1]
        if part == 0:
            pl.semaphore_wait(barrier, count - 1)

        @pl.loop(0, layers)
        def _(turn):
            other = lax.rem(home + turn, layers) * per_mode + part
            step = wrap(other - me + count)

            @pl.when(step != 0)
            def _():
                exchange(moments, gathered, send_a, recv_a, step).start()

    edge_copy(0).start()
    edge_copy(1).start()
    save = pltpu.make_async_copy(field, field_out, local.at[0])
    save.start()
    gathered[me] = moments[me]
    mine = eigen[0:1, 0:piece]
    for part in range(1, per_mode):
        mine = jnp.where(me % per_mode == part, eigen[0:1, part * piece : (part + 1) * piece], mine)
    own, _, _ = roots(mine + radii[me // per_mode])
    stride = power(own, rows)
    whole = power(own, count * rows + 1)
    scale = 1.0 / (1.0 - whole * whole)

    @pl.loop(1, count)
    def _(step):
        exchange(moments, gathered, send_a, recv_a, step).wait_recv()

    total_ahead = gathered[0, 0:1, :]
    for p in range(1, count):
        total_ahead = total_ahead * stride + gathered[p, 0:1, :]
    total_ahead = total_ahead * own
    total_behind = gathered[count - 1, 1:2, :]
    for p in range(count - 2, -1, -1):
        total_behind = total_behind * stride + gathered[p, 1:2, :]
    first = (total_ahead * whole - total_behind) * scale
    last = (total_behind * whole - total_ahead) * scale * own
    for p in range(count):
        solved[p, 0:1, :] = first
        first = first * stride + gathered[p, 0:1, :]
    for p in range(count - 1, -1, -1):
        solved[p, 1:2, :] = last
        last = last * stride + gathered[p, 1:2, :]

    @pl.loop(1, count)
    def _(step):
        exchange(solved, landed, send_b, recv_b, step).start()

    landed[me] = solved[me]
    edge_copy(0).wait()
    edge_copy(1).wait()
    vortex_edge[0] = jnp.where(me == 0, 0.0, edge_landed[0])
    vortex_edge[1] = jnp.where(me == count - 1, 0.0, edge_landed[1])

    @pl.loop(1, count)
    def _(step):
        exchange(solved, landed, send_b, recv_b, step).wait_recv()

    for mode in range(layers):
        for part in range(per_mode):
            span = slice(part * piece, (part + 1) * piece)
            carried[0, mode : mode + 1, span] = landed[mode * per_mode + part, 0:1, :]
            carried[1, mode : mode + 1, span] = landed[mode * per_mode + part, 1:2, :]

    @pl.loop(1, count)
    def _(step):
        exchange(moments, gathered, send_a, recv_a, step).wait_send()
        exchange(solved, landed, send_b, recv_b, step).wait_send()

    save.wait()


def backward_kernel(
    sizes, field, carried, vortex_edge, vortex, wind, mask, to_layer, radii, eigen,
    sine_high_in, sine_low_in,
    fresh_out, stream,
    both, stream_pad, vortex_pad, turn, cross, cross_edge,
    sine_high, sine_low, fresh, partial, damp, local, sent, saved,
):
    groups, tiles, layers, rows, width, piece = sizes
    count = groups * tiles
    me = lax.axis_index("group") * tiles + lax.axis_index("tile")
    top = 8
    loads = [
        pltpu.make_async_copy(sine_high_in, sine_high, local.at[0]),
        pltpu.make_async_copy(sine_low_in, sine_low, local.at[1]),
        pltpu.make_async_copy(vortex, vortex_pad.at[:, pl.ds(top, rows), :], local.at[2]),
    ]
    for load in loads:
        load.start()
    shift = radius_column(radii, layers) + eigen[...]
    rho, inverse, spread = roots(shift)
    factor = -0.5 / spread

    def keep(slot, value):
        upper, lower = halves(value * factor)
        both[slot * layers : (slot + 1) * layers, :] = upper
        slot = slot + rows + 2
        both[slot * layers : (slot + 1) * layers, :] = lower

    ahead = carried[0]
    for y in range(rows):
        ahead = ahead * rho + field[y]
        turn[y] = ahead
    behind = carried[1]
    keep(rows + 1, jnp.where(me == count - 1, 0.0, ahead * rho + behind * inverse))
    for y in range(rows - 1, -1, -1):
        keep(y, turn[y] + behind)
        behind = (behind + field[y]) * rho
    keep(rows, jnp.where(me == 0, 0.0, carried[0] + behind))

    chunk = min(rows, 16)
    loads[0].wait()
    loads[1].wait()
    sine = (sine_high[...], sine_low[...])
    mixer = spread_matrix(to_layer[...], chunk, False)

    def store(part):
        return pltpu.make_async_copy(
            stream_pad.at[:, pl.ds(top + part * chunk, chunk), :],
            stream.at[:, pl.ds(part * chunk, chunk), :],
            sent.at[part],
        )

    modes = dot3(both[...], sine)
    for part in range(rows // chunk):
        span = slice(part * chunk * layers, (part + 1) * chunk * layers)
        mixed = dot3(mixer, halves(modes[span])).reshape(layers, chunk, width)
        stream_pad[:, top + part * chunk : top + (part + 1) * chunk, :] = mixed
        store(part).start()
    outer = modes[rows * layers :]
    plain = jnp.concatenate(halves(to_layer[...]), axis=0)
    lane = lax.broadcasted_iota(jnp.int32, (max(rows, layers), width), 1)

    def east_west(value):
        lanes = lane[: value.shape[0]]
        east = jnp.where(lanes == width - 1, 0.0, pltpu.roll(value, width - 1, 1))
        west = jnp.where(lanes == 0, 0.0, pltpu.roll(value, 1, 1))
        return east, west

    for side, row in ((0, top - 1), (1, top + rows)):
        s_edge = dot3(plain, halves(outer[side * layers : (side + 1) * layers]))
        q_edge = vortex_edge[side]
        s_east, s_west = east_west(s_edge)
        q_east, q_west = east_west(q_edge)
        cross_edge[side] = q_edge * (s_east - s_west) - s_edge * (q_east - q_west)
        stream_pad[:, row, :] = s_edge
        vortex_pad[:, row, :] = q_edge
    loads[2].wait()

    def finish(layer):
        return pltpu.make_async_copy(fresh.at[layer], fresh_out.at[layer], saved.at[layer])

    damp[...] = mask[...].astype(jnp.float32) * time_step

    block = 8

    @pl.loop(0, layers)
    def _(layer):
        cross[top - 1 : top, :] = cross_edge[0, pl.ds(layer, 1), :]
        cross[top + rows : top + rows + 1, :] = cross_edge[1, pl.ds(layer, 1), :]
        for start in range(top, top + rows, block):
            here = slice(start, start + block)
            north, south = slice(start + 1, start + block + 1), slice(start - 1, start + block - 1)
            s_mid, q_mid = stream_pad[layer, here, :], vortex_pad[layer, here, :]
            s_east, s_west = east_west(s_mid)
            q_east, q_west = east_west(q_mid)
            s_across = s_east - s_west
            q_across = q_east - q_west
            cross[here, :] = q_mid * s_across - s_mid * q_across
            s_up = stream_pad[layer, north, :] - stream_pad[layer, south, :]
            q_up = vortex_pad[layer, north, :] - vortex_pad[layer, south, :]
            p_east, p_west = east_west(s_mid * q_up - q_mid * s_up)
            partial[start - top : start - top + block, :] = (
                (s_across * q_up - s_up * q_across + (p_east - p_west)) * (1.0 / 12.0)
                + (beta_plane * 0.5) * s_across
            )
        for start in range(top, top + rows, block):
            here = slice(start, start + block)
            north, south = slice(start + 1, start + block + 1), slice(start - 1, start + block - 1)
            out = slice(start - top, start - top + block)
            loss = partial[out, :] + (cross[north, :] - cross[south, :]) * (1.0 / 12.0)
            fresh[layer, out, :] = vortex_pad[layer, here, :] - damp[out, :] * loss

        @pl.when(layer == 0)
        def _():
            fresh[layer] = fresh[layer] + damp[...] * wind[...]

        @pl.when(layer == layers - 1)
        def _():
            s_mid = stream_pad[layer, top : top + rows, :]
            s_east, s_west = east_west(s_mid)
            s_north = stream_pad[layer, top + 1 : top + rows + 1, :]
            s_south = stream_pad[layer, top - 1 : top + rows - 1, :]
            laplace = s_north + s_south + s_east + s_west - 4.0 * s_mid
            fresh[layer] = fresh[layer] - (bottom_drag * damp[...]) * laplace

        finish(layer).start()

    @pl.loop(0, layers)
    def _(layer):
        finish(layer).wait()

    for part in range(rows // chunk):
        store(part).wait()


def body(groups, tiles, vorticity, layer_to_mode, mode_to_layer, inverse_radii, wind, mask):
    layers, rows, width = vorticity.shape
    count = groups * tiles
    piece = layers * width // count
    sizes = (groups, tiles, layers, rows, width, piece)
    sine_high, sine_low = (jnp.asarray(part) for part in sine_parts(width))
    eigen = jnp.asarray(eigen_values(width)[None])
    limit = 56 * 1024 * 1024
    f32, bf16 = jnp.float32, jnp.bfloat16
    dma = pltpu.SemaphoreType.DMA
    field, carried, vortex_edge = pl.pallas_call(
        functools.partial(forward_kernel, sizes),
        out_shape=(
            jax.ShapeDtypeStruct((rows, layers, width), f32),
            jax.ShapeDtypeStruct((2, layers, width), f32),
            jax.ShapeDtypeStruct((2, layers, width), f32),
        ),
        in_specs=[ANY, VMEM, SMEM, VMEM, ANY, ANY],
        out_specs=(ANY, VMEM, VMEM),
        scratch_shapes=[
            pltpu.VMEM((layers, rows, width), f32),
            pltpu.VMEM((width, width), bf16),
            pltpu.VMEM((width, width), bf16),
            pltpu.VMEM((rows, layers, width), f32),
            pltpu.VMEM((2 * rows * layers, width), bf16),
            dma((3,)),
            pltpu.VMEM((2, layers, width), f32),
            pltpu.VMEM((count, 2, piece), f32),
            pltpu.VMEM((count, 2, piece), f32),
            pltpu.VMEM((count, 2, piece), f32),
            pltpu.VMEM((count, 2, piece), f32),
            pltpu.VMEM((2, layers, width), f32),
            dma((count,)), dma((count,)), dma((count,)), dma((count,)), dma((2,)), dma((2,)),
        ],
        compiler_params=pltpu.CompilerParams(
            collective_id=0, has_side_effects=True, vmem_limit_bytes=limit
        ),
        name="forward",
    )(vorticity, layer_to_mode, inverse_radii, eigen, sine_high, sine_low)
    total = (rows + 2) * layers
    return pl.pallas_call(
        functools.partial(backward_kernel, sizes),
        out_shape=(
            jax.ShapeDtypeStruct((layers, rows, width), f32),
            jax.ShapeDtypeStruct((layers, rows, width), f32),
        ),
        in_specs=[VMEM] * 3 + [ANY] + [VMEM] * 3 + [SMEM, VMEM, ANY, ANY],
        out_specs=(ANY, ANY),
        scratch_shapes=[
            pltpu.VMEM((2 * total, width), bf16),
            pltpu.VMEM((layers, rows + 16, width), f32),
            pltpu.VMEM((layers, rows + 16, width), f32),
            pltpu.VMEM((rows, layers, width), f32),
            pltpu.VMEM((rows + 16, width), f32),
            pltpu.VMEM((2, layers, width), f32),
            pltpu.VMEM((width, width), bf16),
            pltpu.VMEM((width, width), bf16),
            pltpu.VMEM((layers, rows, width), f32),
            pltpu.VMEM((rows, width), f32),
            pltpu.VMEM((rows, width), f32),
            dma((3,)), dma((rows // min(rows, 16),)), dma((layers,)),
        ],
        compiler_params=pltpu.CompilerParams(vmem_limit_bytes=limit),
        name="backward",
    )(
        field, carried, vortex_edge, vorticity, wind, mask, mode_to_layer, inverse_radii,
        eigen, sine_high, sine_low,
    )


def solution(mesh):
    groups, tiles = mesh.shape["group"], mesh.shape["tile"]
    rows = P(None, ("group", "tile"), None)
    plane = P(("group", "tile"), None)
    return jax.shard_map(
        functools.partial(body, groups, tiles),
        mesh=mesh,
        in_specs=(rows, P(), P(), P(), plane, plane),
        out_specs=(rows, rows),
        check_vma=False,
    )
```
